768 devices in a mesh: sub: 64 (over z_hi, y, core), grp: 12 (over z_lo, x).
Axes of the slice: x: 4, y: 8, z: 12 (z_hi: 4, z_lo: 3; z = z_hi * 3 + z_lo), core: 2. Of those that a mesh axis runs over, the one named last changes fastest.
Arguments:
- impedance: bfloat16 [64, 12, 2048, 512], P('sub', 'grp'), may hold values from -0.125 to 0.125
- incident: bfloat16 [64, 12, 96, 512], P('sub', 'grp'), may hold values from -6 to 6
- face_order: int32 [64, 12, 192], P('sub', 'grp'), may hold values from 0 to 191, each once within a row
- near_tiles: bfloat16 [64, 12, 3, 128, 128], P('sub', 'grp'), may hold values from -0.3125 to 0.3125
- basis_right: bfloat16 [64, 12, 128, 128], P('sub', 'grp'), may hold values from -0.078125 to 0.078125
- rank_scale: float32 [64, 128], P('sub'), may hold values from 0.3 to 3
- rank_counts: int32 [16], replicated, may hold values from 32 to 128
- coupling: bfloat16 [64, 16, 128, 128], P('sub'), may hold values from -0.0625 to 0.0625
- basis_left: bfloat16 [64, 12, 128, 128], P('sub', 'grp'), may hold values from -0.5 to 0.5
Outputs:
- traces: bfloat16 [64, 12, 96, 512], P('sub', 'grp')
The draws below stay inside these ranges and needn't reach their ends.
Inputs may be any that keep to these rules, and one draw needn't show every extreme that they name: `face_order`: each row is a permutation of 0 to 191.
All inputs are finite; a program needn't handle non-finite values.
Results may differ from the reference program's by a relative error of at most 0.012.
Values may be sent and summed in bfloat16 or wider, within the bound.
No kernel may reach another device: no remote copies, remote signals or barrier semaphores. Data moves between devices by JAX's collectives and lax.ppermute only.
A program may use at most 32 MiB of HBM per device.

```python
import math
from functools import partial
import jax
import jax.numpy as jnp
from jax import lax

ORDER = 2048
QUARTER = 512
FACE_Q = 192
OUTER_Q = 128
RANK = 128
EXC = 96
ITERS = 3
LAYERS = 16
N_SUB = 64
N_GRP = 12


def place_ends(result, stream_key, low, top_value):
    shape = result.shape
    place = [jax.random.randint(jax.random.fold_in(stream_key, axis), (), 0, shape[axis]) for axis in range(len(shape))]
    result = result.at[tuple(place)].set(low)
    longest = shape.index(max(shape))
    place[longest] = (place[longest] + 1) % shape[longest]
    return result.at[tuple(place)].set(top_value)


def block_levels(stream_key, extent, shards, smallest, high):
    factor_of = 1.0
    for axis_at, shards_of in shards:
        steps = jax.random.uniform(jax.random.fold_in(jax.random.fold_in(stream_key, 6), axis_at), (shards_of,), jnp.float32, smallest / len(shards), high / len(shards))
        factor_of = factor_of * jnp.repeat(jnp.exp(steps), extent[axis_at] // shards_of).reshape((-1,) + (1,) * (len(extent) - 1 - axis_at))
    return factor_of


def bell_draw(stream_key, extent, scale, most, cuts=(), held_as=jnp.bfloat16):
    result = scale * jax.random.normal(stream_key, extent, jnp.float32)
    if cuts:
        result = result * block_levels(stream_key, extent, cuts, -0.22, 0.18)
    return jnp.clip(result, -most, most).astype(held_as)


def setup_inputs(seed: int = 0) -> dict:
    arg_keys = jax.random.split(jax.random.key(seed), 10)
    impedance = bell_draw(arg_keys[0], (N_SUB, N_GRP, ORDER, QUARTER), ORDER ** -0.5, 0.125, ((0, 64), (1, 12)))
    incident = bell_draw(arg_keys[1], (N_SUB, N_GRP, EXC, QUARTER), 1.0, 6.0, ((0, 64), (1, 12)))
    face_order = jax.vmap(lambda own: jax.random.permutation(own, FACE_Q))(jax.random.split(arg_keys[2], N_SUB * N_GRP)).reshape((N_SUB, N_GRP, FACE_Q)).astype(jnp.int32)
    near_tiles = bell_draw(arg_keys[3], (N_SUB, N_GRP, 3, OUTER_Q, OUTER_Q), (3 * OUTER_Q) ** -0.5, 0.3125, ((0, 64), (1, 12)))
    basis_right = bell_draw(arg_keys[4], (N_SUB, N_GRP, OUTER_Q, RANK), (4 * N_GRP * OUTER_Q) ** -0.5, 0.078125, ((0, 64), (1, 12)))
    rank_scale = jnp.clip(jnp.exp(math.log(3.0) - 2.3025851 * jax.random.uniform(arg_keys[5], (N_SUB, RANK), jnp.float32) ** block_levels(arg_keys[5], (N_SUB, RANK), ((0, 64),), -0.2, 0.2)), 0.3, 3.0)
    rank_counts = place_ends(jax.random.randint(arg_keys[6], (LAYERS,), RANK // 4, RANK + 1), jax.random.fold_in(arg_keys[6], 1), RANK // 4, RANK).astype(jnp.int32)
    coupling = bell_draw(arg_keys[7], (N_SUB, LAYERS, RANK, RANK), (RANK * N_SUB) ** -0.5, 0.0625, ((0, 64),))
    basis_left = bell_draw(arg_keys[8], (N_SUB, N_GRP, RANK, OUTER_Q), RANK ** -0.5, 0.5, ((0, 64), (1, 12)))
    return {"impedance": impedance, "incident": incident, "face_order": face_order, "near_tiles": near_tiles, "basis_right": basis_right, "rank_scale": rank_scale, "rank_counts": rank_counts, "coupling": coupling, "basis_left": basis_left}


def apply_layer(pair):
    whole, z_block = pair
    return jnp.einsum("gko,qgoc->qgkc", whole.astype(jnp.float32), z_block.astype(jnp.float32))


def far_target(coef_wide, owner, pair):
    couple_rows, mask_row = pair
    chosen = jnp.where(mask_row[:, None, None], couple_rows[owner].astype(jnp.float32), jnp.float32(0.0))
    return jnp.einsum("skr,srt->kt", coef_wide, chosen)


def reference(impedance, incident, face_order, near_tiles, basis_right, rank_scale, rank_counts, coupling, basis_left):
    layers = N_SUB // 4
    owner = (jnp.arange(N_SUB) // 4).astype(jnp.int32)
    kept = jnp.where(jnp.arange(RANK)[None, :] < rank_counts[owner][:, None], rank_scale, jnp.float32(0.0))
    far_mask = owner[:, None] != owner[None, :]
    z_layers = impedance.reshape(layers, 4, N_GRP, ORDER, QUARTER)
    trace_now = incident
    for sweep_index in range(ITERS):
        whole = trace_now.reshape(layers, 4, N_GRP, EXC, QUARTER).transpose(0, 2, 3, 1, 4).reshape(layers, N_GRP, EXC, ORDER)
        outgoing = lax.map(apply_layer, (whole, z_layers)).reshape(N_SUB, N_GRP, EXC, QUARTER).astype(jnp.bfloat16)
        lower_out = outgoing[..., :FACE_Q]
        upper_out = outgoing[..., FACE_Q:2 * FACE_Q]
        outer_out = outgoing[..., 2 * FACE_Q:]
        partial_sum = jnp.einsum("sgko,sgor->skr", outer_out.astype(jnp.float32), basis_right.astype(jnp.float32))
        coefs = (partial_sum * kept[:, None, :]).astype(jnp.bfloat16)
        coef_wide = coefs.astype(jnp.float32)
        far = lax.map(partial(far_target, coef_wide, owner), (coupling, far_mask)).astype(jnp.bfloat16)
        upper_below = jnp.concatenate([jnp.zeros_like(upper_out[:4]), upper_out[:-4]], 0)
        outer_below = jnp.concatenate([jnp.zeros_like(outer_out[:4]), outer_out[:-4]], 0)
        lower_above = jnp.concatenate([lower_out[4:], jnp.zeros_like(lower_out[:4])], 0)
        outer_above = jnp.concatenate([outer_out[4:], jnp.zeros_like(outer_out[:4])], 0)
        index_grid = jnp.broadcast_to(face_order[:, :, None, :], upper_below.shape).astype(jnp.int32)
        lower_in = jnp.take_along_axis(upper_below, index_grid, axis=3)
        tiles = near_tiles.astype(jnp.float32)
        outer_in = jnp.einsum("sgko,sgop->sgkp", outer_out.astype(jnp.float32), tiles[:, :, 0])
        outer_in = outer_in + jnp.einsum("sgko,sgop->sgkp", outer_below.astype(jnp.float32), tiles[:, :, 1])
        outer_in = outer_in + jnp.einsum("sgko,sgop->sgkp", outer_above.astype(jnp.float32), tiles[:, :, 2])
        outer_in = outer_in + jnp.einsum("skr,sgro->sgko", far.astype(jnp.float32), basis_left.astype(jnp.float32))
        joined = jnp.concatenate([lower_in.astype(jnp.float32), lower_above.astype(jnp.float32), outer_in], 3)
        trace_now = (joined + incident.astype(jnp.float32)).astype(jnp.bfloat16)
    return trace_now
```

```python
import jax
import jax.numpy as jnp
from jax import lax
from jax.sharding import Mesh, PartitionSpec as P

FACE_Q = 192
ITERS = 3
F32, BF16 = jnp.float32, jnp.bfloat16

LAYER = ("zh", "yh")
QUARTER = ("yl", "core")
SUB = LAYER + QUARTER
GRP = ("zl", "x")


def dot(a, b):
    return jnp.dot(a, b, preferred_element_type=F32)


def side_by_side(pieces):
    return jnp.concatenate([pieces[i] for i in range(pieces.shape[0])], axis=-1)


def copies_to(value, axes):
    copies = jnp.broadcast_to(value, (lax.axis_size(axes), *value.shape))
    return lax.all_to_all(copies, axes, 0, 0, tiled=True)


def shifted(value, steps):
    count = lax.axis_size(SUB)
    first, last = max(0, -steps), min(count, count - steps)
    return lax.ppermute(value, SUB, [(s, s + steps) for s in range(first, last)])


def per_device(
    impedance,
    incident,
    face_order,
    near_tiles,
    basis_right,
    rank_scale,
    rank_counts,
    coupling,
    basis_left,
):
    z_cols = impedance[0, 0]
    source = incident[0, 0]
    tiles = near_tiles[0, 0]
    right_basis = basis_right[0, 0]
    left_basis = basis_left[0, 0]
    n_layers, rank, _ = coupling.shape[1:]
    n_exc, width = source.shape
    layer = lax.axis_index(LAYER)
    quarter = lax.axis_index(QUARTER)
    n_q = lax.axis_size(QUARTER)
    n_g = lax.axis_size(GRP)
    rows = n_exc // n_q

    near = lax.all_gather(source, QUARTER)
    y_now = dot(side_by_side(near), z_cols)

    kept = jnp.where(jnp.arange(rank) < rank_counts[layer], rank_scale[0], F32(0.0))
    others = (jnp.arange(n_layers) != layer)[:, None, None]
    own = jnp.where(others, coupling[0], jnp.zeros_like(coupling[0]))
    own = jnp.concatenate([own.reshape(n_layers * rank, rank), left_basis], 0)
    of_all = copies_to(own, QUARTER)
    couple = side_by_side(of_all[:, : n_layers * rank])
    left = of_all[:, n_layers * rank :]
    z_outer = z_cols.reshape(n_q, width, width)[:, 2 * FACE_Q :]
    far_to_y = jnp.einsum("qrt,qtc->qrc", left, z_outer, preferred_element_type=F32)
    far_to_y = far_to_y.reshape(n_q * rank, width).astype(BF16)
    reorder = jax.nn.one_hot(face_order[0, 0], FACE_Q, axis=0, dtype=BF16)

    for sweep in range(ITERS):
        outgoing = y_now.astype(BF16)
        outer_out = outgoing[:, 2 * FACE_Q :]
        partial = (dot(outer_out, right_basis) * kept).astype(BF16)
        parts = jnp.broadcast_to(
            partial.reshape(n_q, 1, rows, rank), (n_q, n_g, rows, rank)
        ).reshape(n_q * n_g, rows, rank)
        arrived = lax.all_to_all(parts, QUARTER + GRP, 0, 0, tiled=True)
        below = shifted(outgoing[:, FACE_Q:], 4)
        above = shifted(jnp.concatenate([outgoing[:, :FACE_Q], outer_out], 1), -4)
        coefs = arrived.astype(F32).sum(0).astype(BF16)
        of_layers = copies_to(coefs, LAYER)
        lower_in = dot(below[:, :FACE_Q], reorder)
        lower_above = above[:, :FACE_Q].astype(F32)
        outer_in = dot(outer_out, tiles[0]) + dot(below[:, FACE_Q:], tiles[1])
        outer_in = outer_in + dot(above[:, FACE_Q:], tiles[2])
        near = jnp.concatenate([lower_in, lower_above, outer_in], 1) + source.astype(F32)
        far = dot(side_by_side(of_layers), couple).astype(BF16)
        if sweep < ITERS - 1:
            both = jnp.concatenate([near.astype(BF16), far], 0)
            both = lax.all_gather(both, QUARTER)
            far = both[:, n_exc:].reshape(n_exc, width)
            y_now = dot(side_by_side(both[:, :n_exc]), z_cols) + dot(far, far_to_y)
        else:
            far = lax.all_gather(far, QUARTER).reshape(n_exc, width)
            far = lax.dynamic_slice_in_dim(far, quarter * rank, rank, 1)
            far = dot(far, left_basis)
            outer = near[:, 2 * FACE_Q :] + far
            trace = jnp.concatenate([near[:, : 2 * FACE_Q], outer], 1)
    return trace.astype(BF16)[None, None]


def solution(mesh):
    finer = Mesh(mesh.devices.reshape(4, 4, 2, 2, 3, 4), SUB + GRP)
    placed = (
        P(SUB, GRP, None, None),
        P(SUB, GRP, None, None),
        P(SUB, GRP, None),
        P(SUB, GRP, None, None, None),
        P(SUB, GRP, None, None),
        P(SUB, None),
        P(),
        P(SUB, None, None, None),
        P(SUB, GRP, None, None),
    )
    return jax.shard_map(
        per_device,
        mesh=finer,
        in_specs=placed,
        out_specs=P(SUB, GRP, None, None),
        check_vma=False,
    )
```

```python
import jax
import jax.numpy as jnp
from jax import lax
from jax.sharding import Mesh, PartitionSpec as P

FACE_Q = 192
ITERS = 3
F32, BF16 = jnp.float32, jnp.bfloat16

LAYER = ("zh", "yh")
QUARTER = ("yl", "core")
SUB = LAYER + QUARTER
GRP = ("zl", "x")
FIRST = QUARTER + ("x",)
SECOND = LAYER + ("zl",)


def dot(a, b):
    return jnp.dot(a, b, preferred_element_type=F32)


def side_by_side(pieces):
    return jnp.concatenate([pieces[i] for i in range(pieces.shape[0])], axis=-1)


def from_other(value, axis):
    return lax.ppermute(value, axis, [(0, 1), (1, 0)])


def in_order(flip, pair):
    mine, other = pair
    return jnp.where(flip, other, mine), jnp.where(flip, mine, other)


def shifted(value, steps):
    count = lax.axis_size(SUB)
    first, last = max(0, -steps), min(count, count - steps)
    return lax.ppermute(value, SUB, [(s, s + steps) for s in range(first, last)])


def per_device(
    impedance,
    incident,
    face_order,
    near_tiles,
    basis_right,
    rank_scale,
    rank_counts,
    coupling,
    basis_left,
):
    z_cols = impedance[0, 0]
    source = incident[0, 0]
    tiles = near_tiles[0, 0]
    right_basis = basis_right[0, 0]
    left_basis = basis_left[0, 0]
    n_layers, rank, _ = coupling.shape[1:]
    n_exc, width = source.shape
    layer = lax.axis_index(LAYER)
    quarter = lax.axis_index(QUARTER)
    n_q = lax.axis_size(QUARTER)
    n_x, n_zl = lax.axis_size("x"), lax.axis_size("zl")
    rows = n_exc // n_q

    near = lax.all_gather(source, QUARTER)
    y_now = dot(side_by_side(near), z_cols)

    kept = jnp.where(jnp.arange(rank) < rank_counts[layer], rank_scale[0], F32(0.0))
    others = (jnp.arange(n_layers) != layer)[:, None, None]
    own = jnp.where(others, coupling[0], jnp.zeros_like(coupling[0]))
    own = jnp.concatenate([own.reshape(n_layers * rank, rank), left_basis], 0)
    yl, core = lax.axis_index("yl"), lax.axis_index("core")
    chips = jnp.stack([own, from_other(own, "yl")])
    of_all = jnp.stack([chips, from_other(chips, "core")], 1)
    of_all = of_all.reshape(n_q, n_layers * rank + rank, rank)
    couple = side_by_side(of_all[:, : n_layers * rank])
    left = of_all[:, n_layers * rank :]

    def by_quarter(blocks):
        upper = in_order(core == 1, (blocks[0], blocks[1]))
        lower = in_order(core == 1, (blocks[2], blocks[3]))
        first = in_order(yl == 1, (upper[0], lower[0]))
        second = in_order(yl == 1, (upper[1], lower[1]))
        return first[0], second[0], first[1], second[1]

    left = jnp.stack(by_quarter(left))
    z_outer = z_cols.reshape(n_q, width, width)[:, 2 * FACE_Q :]
    far_to_y = jnp.einsum("qrt,qtc->qrc", left, z_outer, preferred_element_type=F32)
    far_to_y = far_to_y.reshape(n_q * rank, width).astype(BF16)
    reorder = jax.nn.one_hot(face_order[0, 0], FACE_Q, axis=0, dtype=BF16)

    for sweep in range(ITERS):
        outgoing = y_now.astype(BF16)
        outer_out = outgoing[:, 2 * FACE_Q :]
        partial = (dot(outer_out, right_basis) * kept).astype(BF16)
        parts = jnp.broadcast_to(
            partial.reshape(n_q, 1, rows, rank), (n_q, n_x, rows, rank)
        ).reshape(n_q * n_x, rows, rank)
        arrived = lax.all_to_all(parts, FIRST, 0, 0, tiled=True)
        coefs = arrived.astype(F32).sum(0).astype(BF16)
        copies = jnp.broadcast_to(coefs, (n_layers * n_zl, rows, rank))
        copies, outgoing = lax.optimization_barrier((copies, outgoing))
        outer_out = outgoing[:, 2 * FACE_Q :]
        of_layers = lax.all_to_all(copies, SECOND, 0, 0, tiled=True)
        of_layers = of_layers.reshape(n_layers, n_zl, rows, rank)
        of_layers = of_layers.astype(F32).sum(1).astype(BF16)
        below = shifted(outgoing[:, FACE_Q:], 4)
        above = shifted(jnp.concatenate([outgoing[:, :FACE_Q], outer_out], 1), -4)
        lower_in = dot(below[:, :FACE_Q], reorder)
        lower_above = above[:, :FACE_Q].astype(F32)
        outer_in = dot(outer_out, tiles[0]) + dot(below[:, FACE_Q:], tiles[1])
        outer_in = outer_in + dot(above[:, FACE_Q:], tiles[2])
        near = jnp.concatenate([lower_in, lower_above, outer_in], 1) + source.astype(F32)
        far = dot(of_layers.transpose(1, 0, 2).reshape(rows, -1), couple)
        far = [far[:, k * rank : (k + 1) * rank] for k in range(n_q)]
        far = jnp.concatenate(by_quarter(far), 1).astype(BF16)
        if sweep < ITERS - 1:
            both = jnp.concatenate([near.astype(BF16), far], 0)
            both = lax.all_gather(both, QUARTER)
            far = both[:, n_exc:].reshape(n_exc, width)
            y_now = dot(side_by_side(both[:, :n_exc]), z_cols) + dot(far, far_to_y)
        else:
            far = lax.all_gather(far, QUARTER).reshape(n_exc, width)
            far = lax.dynamic_slice_in_dim(far, quarter * rank, rank, 1)
            far = dot(far, left_basis)
            outer = near[:, 2 * FACE_Q :] + far
            trace = jnp.concatenate([near[:, : 2 * FACE_Q], outer], 1)
    return trace.astype(BF16)[None, None]


def solution(mesh):
    finer = Mesh(mesh.devices.reshape(4, 4, 2, 2, 3, 4), SUB + GRP)
    placed = (
        P(SUB, GRP, None, None),
        P(SUB, GRP, None, None),
        P(SUB, GRP, None),
        P(SUB, GRP, None, None, None),
        P(SUB, GRP, None, None),
        P(SUB, None),
        P(),
        P(SUB, None, None, None),
        P(SUB, GRP, None, None),
    )
    return jax.shard_map(
        per_device,
        mesh=finer,
        in_specs=placed,
        out_specs=P(SUB, GRP, None, None),
        check_vma=False,
    )
```

```python
import jax
import jax.numpy as jnp
from jax import lax
from jax.sharding import Mesh, PartitionSpec as P

FACE_Q = 192
ITERS = 3
F32, BF16 = jnp.float32, jnp.bfloat16

LAYER = ("zh", "yh")
QUARTER = ("yl", "core")
SUB = LAYER + QUARTER
GRP = ("zl", "x")


def dot(a, b):
    return jnp.dot(a, b, preferred_element_type=F32)


def side_by_side(pieces):
    return jnp.concatenate([pieces[i] for i in range(pieces.shape[0])], axis=-1)


def from_other(value, axis):
    return lax.ppermute(value, axis, [(0, 1), (1, 0)])


def in_order(flip, pair):
    mine, other = pair
    return jnp.where(flip, other, mine), jnp.where(flip, mine, other)


def with_neighbours(value, first):
    n_q = lax.axis_size(QUARTER)
    pairs = []
    for lower in range(first, lax.axis_size(LAYER) - 1, 2):
        for q in range(n_q):
            here, there = lower * n_q + q, (lower + 1) * n_q + q
            pairs += [(here, there), (there, here)]
    return lax.ppermute(value, SUB, pairs)


def per_device(
    impedance,
    incident,
    face_order,
    near_tiles,
    basis_right,
    rank_scale,
    rank_counts,
    coupling,
    basis_left,
):
    z_cols = impedance[0, 0]
    source = incident[0, 0]
    tiles = near_tiles[0, 0]
    right_basis = basis_right[0, 0]
    left_basis = basis_left[0, 0]
    n_layers, rank, _ = coupling.shape[1:]
    n_exc, width = source.shape
    layer = lax.axis_index(LAYER)
    quarter = lax.axis_index(QUARTER)
    n_q = lax.axis_size(QUARTER)
    n_g = lax.axis_size(GRP)
    rows = n_exc // n_q

    yl, core = lax.axis_index("yl"), lax.axis_index("core")
    even = layer % 2 == 0

    flat = side_by_side(left_basis.reshape(-1, rank * rank // width, rank))
    both = lax.all_gather(jnp.concatenate([source, flat], 0), QUARTER)
    own, both = lax.optimization_barrier((coupling[0], both))
    own = own.reshape(n_layers * rank, rank)
    other = from_other(own, "yl")
    y_now = dot(side_by_side(both[:, :n_exc]), z_cols)
    left = both[:, n_exc:].reshape(n_q, -1, width // rank, rank)
    left = left.transpose(0, 2, 1, 3).reshape(n_q, rank, rank)

    kept = jnp.where(jnp.arange(rank) < rank_counts[layer], rank_scale[0], F32(0.0))
    others = (jnp.arange(n_layers) != layer)[:, None, None]
    z_outer = z_cols.reshape(n_q, width, width)[:, 2 * FACE_Q :]
    far_to_y = jnp.einsum("qrt,qtc->qrc", left, z_outer, preferred_element_type=F32)
    far_to_y = far_to_y.reshape(n_q * rank, width).astype(BF16)
    reorder = jax.nn.one_hot(face_order[0, 0], FACE_Q, axis=0, dtype=BF16)

    def by_quarter(blocks):
        upper = in_order(core == 1, (blocks[0], blocks[1]))
        lower = in_order(core == 1, (blocks[2], blocks[3]))
        first = in_order(yl == 1, (upper[0], lower[0]))
        second = in_order(yl == 1, (upper[1], lower[1]))
        return first[0], second[0], first[1], second[1]

    for sweep in range(ITERS):
        outgoing = y_now.astype(BF16)
        outer_out = outgoing[:, 2 * FACE_Q :]
        partial = (dot(outer_out, right_basis) * kept).astype(BF16)
        parts = jnp.broadcast_to(
            partial.reshape(n_q, 1, rows, rank), (n_q, n_g, rows, rank)
        ).reshape(n_q * n_g, rows, rank)
        up = outgoing[:, FACE_Q:]
        down = jnp.concatenate([outgoing[:, :FACE_Q], outer_out], 1)
        arrived = lax.all_to_all(parts, QUARTER + GRP, 0, 0, tiled=True)
        coefs = arrived.astype(F32).sum(0).astype(BF16)
        if sweep == 0:
            other, coefs = lax.optimization_barrier((other, coefs))
            chips = jnp.stack([own, other])
            of_all = jnp.stack([chips, from_other(chips, "core")], 1)
            couple = side_by_side(of_all.reshape(n_q, n_layers * rank, rank))
        one = with_neighbours(jnp.where(even, up, down), 0)
        two = with_neighbours(jnp.where(even, down, up), 1)
        below, above = jnp.where(even, two, one), jnp.where(even, one, two)
        lower_in = dot(below[:, :FACE_Q], reorder)
        lower_above = above[:, :FACE_Q].astype(F32)
        outer_in = dot(outer_out, tiles[0]) + dot(below[:, FACE_Q:], tiles[1])
        outer_in = outer_in + dot(above[:, FACE_Q:], tiles[2])
        near = jnp.concatenate([lower_in, lower_above, outer_in], 1) + source.astype(F32)
        if sweep < ITERS - 1:
            near = near.astype(BF16)
        copies = jnp.broadcast_to(coefs, (n_layers, rows, rank))
        copies, near = lax.optimization_barrier((copies, near))
        of_layers = lax.all_to_all(copies, LAYER, 0, 0, tiled=True)
        of_layers = jnp.where(others, of_layers, jnp.zeros_like(of_layers))
        far = dot(of_layers.transpose(1, 0, 2).reshape(rows, -1), couple)
        far = [far[:, k * rank : (k + 1) * rank] for k in range(n_q)]
        far = jnp.concatenate(by_quarter(far), 1).astype(BF16)
        if sweep < ITERS - 1:
            both = jnp.concatenate([near, far], 0)
            both = lax.all_gather(both, QUARTER)
            far = both[:, n_exc:].reshape(n_exc, width)
            y_now = dot(side_by_side(both[:, :n_exc]), z_cols) + dot(far, far_to_y)
        else:
            far = lax.all_gather(far, QUARTER).reshape(n_exc, width)
            far = lax.dynamic_slice_in_dim(far, quarter * rank, rank, 1)
            far = dot(far, left_basis)
            outer = near[:, 2 * FACE_Q :] + far
            trace = jnp.concatenate([near[:, : 2 * FACE_Q], outer], 1)
    return trace.astype(BF16)[None, None]


def solution(mesh):
    finer = Mesh(mesh.devices.reshape(4, 4, 2, 2, 3, 4), SUB + GRP)
    placed = (
        P(SUB, GRP, None, None),
        P(SUB, GRP, None, None),
        P(SUB, GRP, None),
        P(SUB, GRP, None, None, None),
        P(SUB, GRP, None, None),
        P(SUB, None),
        P(),
        P(SUB, None, None, None),
        P(SUB, GRP, None, None),
    )
    return jax.shard_map(
        per_device,
        mesh=finer,
        in_specs=placed,
        out_specs=P(SUB, GRP, None, None),
        check_vma=False,
    )
```

```python
import jax
import jax.numpy as jnp
from jax import lax
from jax.sharding import Mesh, PartitionSpec as P

FACE_Q = 192
ITERS = 3
F32, BF16 = jnp.float32, jnp.bfloat16

LAYER = ("zh", "yh")
QUARTER = ("yl", "core")
SUB = LAYER + QUARTER
GRP = ("zl", "x")


def dot(a, b):
    return jnp.dot(a, b, preferred_element_type=F32)


def side_by_side(pieces):
    return jnp.concatenate([pieces[i] for i in range(pieces.shape[0])], axis=-1)


def from_other(value, axis):
    return lax.ppermute(value, axis, [(0, 1), (1, 0)])


def in_order(flip, pair):
    mine, other = pair
    return jnp.where(flip, other, mine), jnp.where(flip, mine, other)


def to_neighbours(value):
    count, step = lax.axis_size(SUB), lax.axis_size(QUARTER)
    pairs = [(s, s + step) for s in range(0, count - step, 2)]
    pairs += [(s, s - step) for s in range(step + 1, count, 2)]
    return lax.ppermute(value, SUB, pairs)


def per_device(
    impedance,
    incident,
    face_order,
    near_tiles,
    basis_right,
    rank_scale,
    rank_counts,
    coupling,
    basis_left,
):
    z_cols = impedance[0, 0]
    source = incident[0, 0]
    tiles = near_tiles[0, 0]
    right_basis = basis_right[0, 0]
    left_basis = basis_left[0, 0]
    n_layers, rank, _ = coupling.shape[1:]
    n_exc, width = source.shape
    layer = lax.axis_index(LAYER)
    quarter = lax.axis_index(QUARTER)
    n_q = lax.axis_size(QUARTER)
    rows = n_exc // n_q
    half = width - FACE_Q

    yl, core = lax.axis_index("yl"), lax.axis_index("core")
    n_x = lax.axis_size("yl") * lax.axis_size(GRP)
    first = core == 0

    flat = side_by_side(left_basis.reshape(-1, rank * rank // width, rank))
    both = lax.all_gather(jnp.concatenate([source, flat], 0), QUARTER)
    own, both = lax.optimization_barrier((coupling[0], both))
    own = own.reshape(n_layers * rank, rank)
    other = from_other(own, "yl")
    y_first = dot(side_by_side(both[:, :n_exc]), z_cols)
    left = both[:, n_exc:].reshape(n_q, -1, width // rank, rank)
    left = left.transpose(0, 2, 1, 3).reshape(n_q, rank, rank)

    kept = jnp.where(jnp.arange(rank) < rank_counts[layer], rank_scale[0], F32(0.0))
    scaled = (right_basis.astype(F32) * kept).astype(BF16)
    order = jnp.pad(face_order[0, 0].astype(BF16), (0, 16 * rank - FACE_Q))
    shared = [scaled, tiles.reshape(3 * rank, rank), order.reshape(16, rank)]
    shared = lax.all_gather(jnp.concatenate(shared, 0), "core")
    scaled = shared[:, :rank]
    passed = jnp.where(first, shared[:, 2 * rank : 3 * rank], shared[:, 3 * rank : 4 * rank])
    order = shared[:, 4 * rank :].reshape(2, -1)[:, :FACE_Q].astype(jnp.int32)
    same = jnp.broadcast_to(jnp.arange(FACE_Q, dtype=jnp.int32), order.shape)
    order = jnp.where(first, order, same)
    reorder = (jnp.arange(FACE_Q)[None, :, None] == order[:, None, :]).astype(BF16)

    others = (jnp.arange(n_layers) != layer)[:, None, None]
    z_quarters = z_cols.reshape(n_q, width, width)
    z_outer = z_quarters[:, 2 * FACE_Q :]
    far_to_y = jnp.einsum("qrt,qtc->qrc", left, z_outer, preferred_element_type=F32)
    far_to_y = far_to_y.reshape(n_q * rank, width).astype(BF16)
    z_near = []
    for chip in (0, 2):
        for face in (0, FACE_Q):
            for q in (chip, chip + 1):
                z_near += [z_quarters[q, face : face + FACE_Q], z_outer[q]]
    z_near = jnp.concatenate(z_near, 0)
    y_now = y_first

    def by_quarter(blocks):
        upper = in_order(core == 1, (blocks[0], blocks[1]))
        lower = in_order(core == 1, (blocks[2], blocks[3]))
        ones = in_order(yl == 1, (upper[0], lower[0]))
        twos = in_order(yl == 1, (upper[1], lower[1]))
        return ones[0], twos[0], ones[1], twos[1]

    for sweep in range(ITERS):
        outgoing = y_now.astype(BF16)
        pair = lax.all_gather(outgoing, "core")
        outer = pair[:, :, 2 * FACE_Q :]
        partial = dot(outer[0], scaled[0]) + dot(outer[1], scaled[1])
        partial = partial.astype(BF16).reshape(n_q // 2, 2, 1, rows, rank)
        partial = jnp.where(first, partial[:, 0], partial[:, 1])
        parts = jnp.broadcast_to(partial, (n_q // 2, 2 * n_x // n_q, rows, rank))
        parts = parts.reshape(n_x, rows, rank)
        arrived = lax.all_to_all(parts, ("yl",) + GRP, 0, 0, tiled=True)
        coefs = arrived.astype(F32).sum(0).astype(BF16)
        faces = jnp.where(first, pair[:, :, FACE_Q : 2 * FACE_Q], pair[:, :, :FACE_Q])
        faces = jnp.concatenate([faces[0], outer[0], faces[1], outer[1]], 1)
        faces = to_neighbours(faces)
        if sweep == 0:
            other, coefs = lax.optimization_barrier((other, coefs))
            chips = jnp.stack([own, other])
            of_all = jnp.stack([chips, from_other(chips, "core")], 1)
            couple = side_by_side(of_all.reshape(n_q, n_layers * rank, rank))
        by_own = dot(outgoing[:, 2 * FACE_Q :], tiles[0])
        near = []
        for k in (0, 1):
            face = faces[:, k * half : k * half + FACE_Q]
            trace = faces[:, k * half + FACE_Q : (k + 1) * half]
            near += [
                dot(face, reorder[k]),
                dot(trace, passed[k]) + jnp.where(core == k, by_own, F32(0.0)),
            ]
        near = jnp.concatenate(near, 1).astype(BF16)
        copies = jnp.broadcast_to(coefs, (n_layers, rows, rank))
        of_layers = lax.all_to_all(copies, LAYER, 0, 0, tiled=True)
        of_layers = jnp.where(others, of_layers, jnp.zeros_like(of_layers))
        far = dot(of_layers.transpose(1, 0, 2).reshape(rows, -1), couple)
        far = [far[:, k * rank : (k + 1) * rank] for k in range(n_q)]
        far = jnp.concatenate(by_quarter(far), 1).astype(BF16)
        if sweep < ITERS - 1:
            far = jnp.pad(far, ((0, 0), (0, 2 * half - width)))
            both = lax.all_gather(jnp.concatenate([near, far], 0), QUARTER)
            far = both[:, n_exc:, :width].reshape(n_exc, width)
            y_now = y_first + dot(side_by_side(both[:, :n_exc]), z_near)
            y_now = y_now + dot(far, far_to_y)
        else:
            near = lax.all_gather(near, "core").astype(F32)
            near = jnp.where(first, near[:, :, :half], near[:, :, half:])
            far = lax.all_gather(far, QUARTER).reshape(n_exc, width)
            far = lax.dynamic_slice_in_dim(far, quarter * rank, rank, 1)
            far = dot(far, left_basis)
            outer_in = near[0, :, FACE_Q:] + near[1, :, FACE_Q:] + far
            faces_in = [near[0, :, :FACE_Q], near[1, :, :FACE_Q]]
            trace = jnp.concatenate([*faces_in, outer_in], 1) + source.astype(F32)
    return trace.astype(BF16)[None, None]


def solution(mesh):
    finer = Mesh(mesh.devices.reshape(4, 4, 2, 2, 3, 4), SUB + GRP)
    placed = (
        P(SUB, GRP, None, None),
        P(SUB, GRP, None, None),
        P(SUB, GRP, None),
        P(SUB, GRP, None, None, None),
        P(SUB, GRP, None, None),
        P(SUB, None),
        P(),
        P(SUB, None, None, None),
        P(SUB, GRP, None, None),
    )
    return jax.shard_map(
        per_device,
        mesh=finer,
        in_specs=placed,
        out_specs=P(SUB, GRP, None, None),
        check_vma=False,
    )
```

```python
import jax
import jax.numpy as jnp
from jax import lax
from jax.sharding import Mesh, PartitionSpec as P

FACE_Q = 192
ITERS = 3
F32, BF16 = jnp.float32, jnp.bfloat16

LAYER = ("zh", "yh")
QUARTER = ("yl", "core")
SUB = LAYER + QUARTER
GRP = ("zl", "x")
FIRST = QUARTER + ("x",)
SECOND = LAYER + ("zl",)


def dot(a, b):
    return jnp.dot(a, b, preferred_element_type=F32)


def side_by_side(pieces):
    return jnp.concatenate([pieces[i] for i in range(pieces.shape[0])], axis=-1)


def from_other(value, axis):
    return lax.ppermute(value, axis, [(0, 1), (1, 0)])


def in_order(flip, pair):
    mine, other = pair
    return jnp.where(flip, other, mine), jnp.where(flip, mine, other)


def shifted(value, steps):
    count = lax.axis_size(SUB)
    first, last = max(0, -steps), min(count, count - steps)
    return lax.ppermute(value, SUB, [(s, s + steps) for s in range(first, last)])


def per_device(
    impedance,
    incident,
    face_order,
    near_tiles,
    basis_right,
    rank_scale,
    rank_counts,
    coupling,
    basis_left,
):
    z_cols = impedance[0, 0]
    source = incident[0, 0]
    tiles = near_tiles[0, 0]
    right_basis = basis_right[0, 0]
    left_basis = basis_left[0, 0]
    n_layers, rank, _ = coupling.shape[1:]
    n_exc, width = source.shape
    layer = lax.axis_index(LAYER)
    quarter = lax.axis_index(QUARTER)
    n_q = lax.axis_size(QUARTER)
    n_x, n_zl = lax.axis_size("x"), lax.axis_size("zl")
    rows = n_exc // n_q

    yl, core = lax.axis_index("yl"), lax.axis_index("core")

    both = jnp.pad(source, ((0, rank - n_exc), (0, 0)))
    both = lax.all_gather(jnp.concatenate([both, left_basis], 1), QUARTER)
    y_now = dot(side_by_side(both[:, :n_exc, :width]), z_cols)
    left = both[:, :, width:]

    kept = jnp.where(jnp.arange(rank) < rank_counts[layer], rank_scale[0], F32(0.0))
    others = (jnp.arange(n_layers) != layer)[:, None, None]
    z_outer = z_cols.reshape(n_q, width, width)[:, 2 * FACE_Q :]
    far_to_y = jnp.einsum("qrt,qtc->qrc", left, z_outer, preferred_element_type=F32)
    far_to_y = far_to_y.reshape(n_q * rank, width).astype(BF16)
    reorder = jax.nn.one_hot(face_order[0, 0], FACE_Q, axis=0, dtype=BF16)

    def by_quarter(blocks):
        upper = in_order(core == 1, (blocks[0], blocks[1]))
        lower = in_order(core == 1, (blocks[2], blocks[3]))
        first = in_order(yl == 1, (upper[0], lower[0]))
        second = in_order(yl == 1, (upper[1], lower[1]))
        return first[0], second[0], first[1], second[1]

    for sweep in range(ITERS):
        outgoing = y_now.astype(BF16)
        outer_out = outgoing[:, 2 * FACE_Q :]
        partial = (dot(outer_out, right_basis) * kept).astype(BF16)
        parts = jnp.broadcast_to(
            partial.reshape(n_q, 1, rows, rank), (n_q, n_x, rows, rank)
        ).reshape(n_q * n_x, rows, rank)
        arrived = lax.all_to_all(parts, FIRST, 0, 0, tiled=True)
        coefs = arrived.astype(F32).sum(0).astype(BF16)
        copies = jnp.broadcast_to(coefs, (n_layers * n_zl, rows, rank))
        copies, outgoing = lax.optimization_barrier((copies, outgoing))
        if sweep == 0:
            copies, own = lax.optimization_barrier((copies, coupling[0]))
            own = own.reshape(n_layers * rank, rank)
            across = from_other(own, "yl")
            couple = [own, from_other(own, "core"), across, from_other(across, "core")]
            couple = jnp.concatenate(couple, 1)
        outer_out = outgoing[:, 2 * FACE_Q :]
        of_layers = lax.all_to_all(copies, SECOND, 0, 0, tiled=True)
        of_layers = of_layers.reshape(n_layers, n_zl, rows, rank)
        of_layers = of_layers.astype(F32).sum(1).astype(BF16)
        of_layers = jnp.where(others, of_layers, jnp.zeros_like(of_layers))
        below = shifted(outgoing[:, FACE_Q:], 4)
        above = shifted(jnp.concatenate([outgoing[:, :FACE_Q], outer_out], 1), -4)
        lower_in = dot(below[:, :FACE_Q], reorder)
        lower_above = above[:, :FACE_Q].astype(F32)
        outer_in = dot(outer_out, tiles[0]) + dot(below[:, FACE_Q:], tiles[1])
        outer_in = outer_in + dot(above[:, FACE_Q:], tiles[2])
        near = jnp.concatenate([lower_in, lower_above, outer_in], 1) + source.astype(F32)
        far = dot(of_layers.transpose(1, 0, 2).reshape(rows, -1), couple)
        far = [far[:, k * rank : (k + 1) * rank] for k in range(n_q)]
        far = jnp.concatenate(by_quarter(far), 1).astype(BF16)
        if sweep < ITERS - 1:
            both = jnp.concatenate([near.astype(BF16), far], 0)
            both = lax.all_gather(both, QUARTER)
            far = both[:, n_exc:].reshape(n_exc, width)
            y_now = dot(side_by_side(both[:, :n_exc]), z_cols) + dot(far, far_to_y)
        else:
            far = lax.all_gather(far, QUARTER).reshape(n_exc, width)
            far = lax.dynamic_slice_in_dim(far, quarter * rank, rank, 1)
            far = dot(far, left_basis)
            outer = near[:, 2 * FACE_Q :] + far
            trace = jnp.concatenate([near[:, : 2 * FACE_Q], outer], 1)
    return trace.astype(BF16)[None, None]


def solution(mesh):
    finer = Mesh(mesh.devices.reshape(4, 4, 2, 2, 3, 4), SUB + GRP)
    placed = (
        P(SUB, GRP, None, None),
        P(SUB, GRP, None, None),
        P(SUB, GRP, None),
        P(SUB, GRP, None, None, None),
        P(SUB, GRP, None, None),
        P(SUB, None),
        P(),
        P(SUB, None, None, None),
        P(SUB, GRP, None, None),
    )
    return jax.shard_map(
        per_device,
        mesh=finer,
        in_specs=placed,
        out_specs=P(SUB, GRP, None, None),
        check_vma=False,
    )
```

```python
import jax
import jax.numpy as jnp
from jax import lax
from jax.sharding import Mesh, PartitionSpec as P

FACE_Q = 192
ITERS = 3
F32, BF16 = jnp.float32, jnp.bfloat16

LAYER = ("zh", "yh")
QUARTER = ("yl", "core")
SUB = LAYER + QUARTER
GRP = ("zl", "x")
FIRST = QUARTER + ("x",)
SECOND = LAYER + ("zl",)


def dot(a, b):
    return jnp.dot(a, b, preferred_element_type=F32)


def side_by_side(pieces):
    return jnp.concatenate([pieces[i] for i in range(pieces.shape[0])], axis=-1)


def from_other(value, axis):
    return lax.ppermute(value, axis, [(0, 1), (1, 0)])


def in_order(flip, pair):
    mine, other = pair
    return jnp.where(flip, other, mine), jnp.where(flip, mine, other)


def shifted(value, steps):
    count = lax.axis_size(SUB)
    first, last = max(0, -steps), min(count, count - steps)
    return lax.ppermute(value, SUB, [(s, s + steps) for s in range(first, last)])


def per_device(
    impedance,
    incident,
    face_order,
    near_tiles,
    basis_right,
    rank_scale,
    rank_counts,
    coupling,
    basis_left,
):
    z_cols = impedance[0, 0]
    source = incident[0, 0]
    tiles = near_tiles[0, 0]
    right_basis = basis_right[0, 0]
    left_basis = basis_left[0, 0]
    n_layers, rank, _ = coupling.shape[1:]
    n_exc, width = source.shape
    layer = lax.axis_index(LAYER)
    quarter = lax.axis_index(QUARTER)
    n_q = lax.axis_size(QUARTER)
    n_x, n_zl = lax.axis_size("x"), lax.axis_size("zl")
    rows = n_exc // n_q

    yl, core = lax.axis_index("yl"), lax.axis_index("core")

    both = jnp.pad(source, ((0, rank - n_exc), (0, 0)))
    both = lax.all_gather(jnp.concatenate([both, left_basis], 1), QUARTER)
    y_now = dot(side_by_side(both[:, :n_exc, :width]), z_cols)
    left = both[:, :, width:]

    ours = jnp.arange(n_layers) == layer
    count = jnp.sum(jnp.where(ours, rank_counts, 0))
    kept = jnp.where(jnp.arange(rank) < count, rank_scale[0], F32(0.0))
    others = ~ours[:, None, None]
    z_outer = z_cols.reshape(n_q, width, width)[:, 2 * FACE_Q :]
    far_to_y = jnp.einsum("qrt,qtc->qrc", left, z_outer, preferred_element_type=F32)
    far_to_y = far_to_y.reshape(n_q * rank, width).astype(BF16)
    reorder = jax.nn.one_hot(face_order[0, 0], FACE_Q, axis=0, dtype=BF16)

    def by_quarter(blocks):
        upper = in_order(core == 1, (blocks[0], blocks[1]))
        lower = in_order(core == 1, (blocks[2], blocks[3]))
        first = in_order(yl == 1, (upper[0], lower[0]))
        second = in_order(yl == 1, (upper[1], lower[1]))
        return first[0], second[0], first[1], second[1]

    for sweep in range(ITERS):
        outgoing = y_now.astype(BF16)
        outer_out = outgoing[:, 2 * FACE_Q :]
        partial = (dot(outer_out, right_basis) * kept).astype(BF16)
        parts = jnp.broadcast_to(
            partial.reshape(n_q, 1, rows, rank), (n_q, n_x, rows, rank)
        ).reshape(n_q * n_x, rows, rank)
        arrived = lax.all_to_all(parts, FIRST, 0, 0, tiled=True)
        coefs = arrived.astype(F32).sum(0).astype(BF16)
        copies = jnp.broadcast_to(coefs, (n_layers * n_zl, rows, rank))
        copies, outgoing = lax.optimization_barrier((copies, outgoing))
        if sweep == 0:
            copies, own = lax.optimization_barrier((copies, coupling[0]))
            own = own.reshape(n_layers * rank, rank)
            across = from_other(own, "yl")
            theirs = from_other(jnp.stack([own, across]), "core")
            couple = jnp.concatenate([own, theirs[0], across, theirs[1]], 1)
            couple = lax.optimization_barrier(couple)
        outer_out = outgoing[:, 2 * FACE_Q :]
        of_layers = lax.all_to_all(copies, SECOND, 0, 0, tiled=True)
        of_layers = of_layers.reshape(n_layers, n_zl, rows, rank)
        of_layers = of_layers.astype(F32).sum(1).astype(BF16)
        of_layers = jnp.where(others, of_layers, jnp.zeros_like(of_layers))
        below = shifted(outgoing[:, FACE_Q:], 4)
        above = shifted(jnp.concatenate([outgoing[:, :FACE_Q], outer_out], 1), -4)
        lower_in = dot(below[:, :FACE_Q], reorder)
        lower_above = above[:, :FACE_Q].astype(F32)
        outer_in = dot(outer_out, tiles[0]) + dot(below[:, FACE_Q:], tiles[1])
        outer_in = outer_in + dot(above[:, FACE_Q:], tiles[2])
        near = jnp.concatenate([lower_in, lower_above, outer_in], 1) + source.astype(F32)
        far = dot(of_layers.transpose(1, 0, 2).reshape(rows, -1), couple)
        far = [far[:, k * rank : (k + 1) * rank] for k in range(n_q)]
        far = jnp.concatenate(by_quarter(far), 1).astype(BF16)
        if sweep < ITERS - 1:
            both = jnp.concatenate([near.astype(BF16), far], 0)
            both = lax.all_gather(both, QUARTER)
            far = both[:, n_exc:].reshape(n_exc, width)
            y_now = dot(side_by_side(both[:, :n_exc]), z_cols) + dot(far, far_to_y)
        else:
            far = lax.all_gather(far, QUARTER).reshape(n_exc, width)
            far = lax.dynamic_slice_in_dim(far, quarter * rank, rank, 1)
            far = dot(far, left_basis)
            outer = near[:, 2 * FACE_Q :] + far
            trace = jnp.concatenate([near[:, : 2 * FACE_Q], outer], 1)
    return trace.astype(BF16)[None, None]


def solution(mesh):
    finer = Mesh(mesh.devices.reshape(4, 4, 2, 2, 3, 4), SUB + GRP)
    placed = (
        P(SUB, GRP, None, None),
        P(SUB, GRP, None, None),
        P(SUB, GRP, None),
        P(SUB, GRP, None, None, None),
        P(SUB, GRP, None, None),
        P(SUB, None),
        P(),
        P(SUB, None, None, None),
        P(SUB, GRP, None, None),
    )
    return jax.shard_map(
        per_device,
        mesh=finer,
        in_specs=placed,
        out_specs=P(SUB, GRP, None, None),
        check_vma=False,
    )
```

```python
import jax
import jax.numpy as jnp
from jax import lax
from jax.sharding import Mesh, PartitionSpec as P

FACE_Q = 192
ITERS = 3
F32, BF16 = jnp.float32, jnp.bfloat16

LAYER = ("zh", "yh")
QUARTER = ("yl", "core")
SUB = LAYER + QUARTER
GRP = ("zl", "x")
FIRST = QUARTER + ("x",)
SECOND = LAYER + ("zl",)


def dot(a, b):
    return jnp.dot(a, b, preferred_element_type=F32)


def side_by_side(pieces):
    return jnp.concatenate([pieces[i] for i in range(pieces.shape[0])], axis=-1)


def from_other(value, axis):
    return lax.ppermute(value, axis, [(0, 1), (1, 0)])


def in_order(flip, pair):
    mine, other = pair
    return jnp.where(flip, other, mine), jnp.where(flip, mine, other)


def shifted(value, steps):
    count = lax.axis_size(SUB)
    first, last = max(0, -steps), min(count, count - steps)
    return lax.ppermute(value, SUB, [(s, s + steps) for s in range(first, last)])


def per_device(
    impedance,
    incident,
    face_order,
    near_tiles,
    basis_right,
    rank_scale,
    rank_counts,
    coupling,
    basis_left,
):
    z_cols = impedance[0, 0]
    source = incident[0, 0]
    tiles = near_tiles[0, 0]
    right_basis = basis_right[0, 0]
    left_basis = basis_left[0, 0]
    n_layers, rank, _ = coupling.shape[1:]
    n_exc, width = source.shape
    layer = lax.axis_index(LAYER)
    quarter = lax.axis_index(QUARTER)
    n_q = lax.axis_size(QUARTER)
    n_x, n_zl = lax.axis_size("x"), lax.axis_size("zl")
    rows = n_exc // n_q

    yl, core = lax.axis_index("yl"), lax.axis_index("core")

    both = jnp.pad(source, ((0, rank - n_exc), (0, 0)))
    both = lax.all_gather(jnp.concatenate([both, left_basis], 1), QUARTER)
    y_now = dot(side_by_side(both[:, :n_exc, :width]), z_cols)
    left = both[:, :, width:]

    ours = jnp.arange(n_layers) == layer
    count = jnp.sum(jnp.where(ours, rank_counts, 0))
    kept = jnp.arange(rank) < count
    others = ~ours[:, None, None]
    z_outer = z_cols.reshape(n_q, width, width)[:, 2 * FACE_Q :]
    far_to_y = jnp.einsum("qrt,qtc->qrc", left, z_outer, preferred_element_type=F32)
    far_to_y = far_to_y.reshape(n_q * rank, width).astype(BF16)
    reorder = jax.nn.one_hot(face_order[0, 0], FACE_Q, axis=0, dtype=BF16)

    def by_quarter(blocks):
        upper = in_order(core == 1, (blocks[0], blocks[1]))
        lower = in_order(core == 1, (blocks[2], blocks[3]))
        first = in_order(yl == 1, (upper[0], lower[0]))
        second = in_order(yl == 1, (upper[1], lower[1]))
        return first[0], second[0], first[1], second[1]

    for sweep in range(ITERS):
        outgoing = y_now.astype(BF16)
        outer_out = outgoing[:, 2 * FACE_Q :]
        partial = (dot(outer_out, right_basis) * rank_scale).astype(BF16)
        parts = jnp.broadcast_to(
            partial.reshape(n_q, 1, rows, rank), (n_q, n_x, rows, rank)
        ).reshape(n_q * n_x, rows, rank)
        arrived = lax.all_to_all(parts, FIRST, 0, 0, tiled=True)
        coefs = jnp.where(kept, arrived.astype(F32).sum(0), F32(0.0)).astype(BF16)
        if sweep == 0:
            coefs, far_to_y = lax.optimization_barrier((coefs, far_to_y))
        copies = jnp.broadcast_to(coefs, (n_layers * n_zl, rows, rank))
        copies, outgoing = lax.optimization_barrier((copies, outgoing))
        if sweep == 0:
            copies, own = lax.optimization_barrier((copies, coupling[0]))
            own = own.reshape(n_layers * rank, rank)
            across = from_other(own, "yl")
            chips = jnp.concatenate([own, across], 1)
            couple = jnp.concatenate([chips, from_other(chips, "core")], 1)
            couple = lax.optimization_barrier(couple)
        outer_out = outgoing[:, 2 * FACE_Q :]
        of_layers = lax.all_to_all(copies, SECOND, 0, 0, tiled=True)
        of_layers = of_layers.reshape(n_layers, n_zl, rows, rank)
        of_layers = of_layers.astype(F32).sum(1).astype(BF16)
        of_layers = jnp.where(others, of_layers, jnp.zeros_like(of_layers))
        below = shifted(outgoing[:, FACE_Q:], 4)
        above = shifted(jnp.concatenate([outgoing[:, :FACE_Q], outer_out], 1), -4)
        lower_in = dot(below[:, :FACE_Q], reorder)
        lower_above = above[:, :FACE_Q].astype(F32)
        outer_in = dot(outer_out, tiles[0]) + dot(below[:, FACE_Q:], tiles[1])
        outer_in = outer_in + dot(above[:, FACE_Q:], tiles[2])
        near = jnp.concatenate([lower_in, lower_above, outer_in], 1) + source.astype(F32)
        far = dot(of_layers.transpose(1, 0, 2).reshape(rows, -1), couple)
        far = [far[:, k * rank : (k + 1) * rank] for k in (0, 2, 1, 3)]
        far = jnp.concatenate(by_quarter(far), 1).astype(BF16)
        if sweep < ITERS - 1:
            both = jnp.concatenate([near.astype(BF16), far], 0)
            both = lax.all_gather(both, QUARTER)
            far = both[:, n_exc:].reshape(n_exc, width)
            y_now = dot(side_by_side(both[:, :n_exc]), z_cols) + dot(far, far_to_y)
        else:
            far = lax.all_gather(far, QUARTER).reshape(n_exc, width)
            far = lax.dynamic_slice_in_dim(far, quarter * rank, rank, 1)
            far = dot(far, left_basis)
            outer = near[:, 2 * FACE_Q :] + far
            trace = jnp.concatenate([near[:, : 2 * FACE_Q], outer], 1)
    return trace.astype(BF16)[None, None]


def solution(mesh):
    finer = Mesh(mesh.devices.reshape(4, 4, 2, 2, 3, 4), SUB + GRP)
    placed = (
        P(SUB, GRP, None, None),
        P(SUB, GRP, None, None),
        P(SUB, GRP, None),
        P(SUB, GRP, None, None, None),
        P(SUB, GRP, None, None),
        P(SUB, None),
        P(),
        P(SUB, None, None, None),
        P(SUB, GRP, None, None),
    )
    return jax.shard_map(
        per_device,
        mesh=finer,
        in_specs=placed,
        out_specs=P(SUB, GRP, None, None),
        check_vma=False,
    )
```
